256 devices in a mesh: box: 64 (over x, z, core), src: 4 (over y).
Axes of the slice: x: 4, y: 4, z: 8, core: 2. Of those that a mesh axis runs over, the one named last changes fastest.
Arguments:
- source_field: bfloat16 [512, 524288], P('src', 'box'), parts along dimension 0, may hold values from -6 to 6
- project_mats: bfloat16 [4096, 128], P('box'), may hold values from -0.5 to 0.5
- local_mats: bfloat16 [8, 2, 4096, 64], P(None, None, 'box'), may hold values from -0.75 to 0.75
- cross_mats: bfloat16 [6, 2, 4096, 64], P(None, None, 'box'), may hold values from -0.75 to 0.75
- angles: bfloat16 [14, 524288], P(None, 'box'), may hold values from -3.140625 to 3.140625
- evaluate_mats: bfloat16 [8192, 64], P('box'), may hold values from -0.75 to 0.75
Outputs:
- image_blocks: bfloat16 [512, 524288], P('src', 'box'), parts along dimension 0
The draws below stay inside these ranges and needn't reach their ends.
There are 4 independent parts, one for each index of `src`. The reference program is written for one: setup_inputs(seed, part) draws one part's arguments, and reference() takes and returns one part's arrays. A program takes and returns all parts, laid end to end along the dimension named above; an argument that names none is the same for every part. Nothing has to cross between parts.
All inputs are finite; a program needn't handle non-finite values.
Results may differ from the reference program's by a relative error of at most 0.024.
Values may be sent and summed in bfloat16 or wider, within the bound.
No kernel may reach another device: no remote copies, remote signals or barrier semaphores. Data moves between devices by JAX's collectives and lax.ppermute only.
A program may use at most 128 MiB of HBM per device.

```python
import jax
import jax.numpy as jnp

R = 64
Q = 128
BOX_DEV = 8192
LOCAL = 8
LEVELS = 6
BOXES = 524288
N_BOX = 64


def level_of(key, extent, cuts, smallest, high):
    loudness, own = 1.0, jax.random.fold_in(key, 6)
    for axis_at, parts in cuts:
        heights = jnp.exp(jax.random.uniform(jax.random.fold_in(own, axis_at), (parts,), jnp.float32, smallest / len(cuts), high / len(cuts)))
        loudness = loudness * jnp.repeat(heights, extent[axis_at] // parts).reshape([-1 if axis == axis_at else 1 for axis in range(len(extent))])
    return loudness


def centred(key, shape, width, bound, cuts=(), kind=jnp.bfloat16):
    drawn = width * jax.random.normal(key, shape, jnp.float32)
    if cuts:
        drawn = drawn * level_of(key, shape, cuts, -0.22, 0.18)
    return jnp.clip(drawn, -bound, bound).astype(kind)


def setup_inputs(seed: int = 0, part: int = 0) -> dict:
    keys = jax.random.split(jax.random.key(seed), 7)
    own_keys = jax.random.split(jax.random.fold_in(keys[6], part), 7)
    return {
        "source_field": centred(own_keys[0], (Q, BOXES), 1.0, 6.0, ((1, 64),)),
        "project_mats": centred(keys[1], (N_BOX * R, Q), Q ** -0.5, 0.5, ((0, 64),)),
        "local_mats": centred(keys[2], (LOCAL, 2, N_BOX * R, R), R ** -0.5, 0.75, ((2, 64),)),
        "cross_mats": centred(keys[3], (LEVELS, 2, N_BOX * R, R), R ** -0.5, 0.75, ((2, 64),)),
        "angles": jnp.clip(jax.random.uniform(keys[4], (LOCAL + LEVELS, BOXES), jnp.float32, -3.140625, 3.140625), -3.140625, 3.140625).astype(jnp.bfloat16),
        "evaluate_mats": centred(keys[5], (N_BOX * Q, R), R ** -0.5, 0.75, ((0, 64),)),
    }


def flip_last(values, pair_span):
    full_shape = values.shape
    leading = full_shape[:-1]
    reshaped = values.reshape(leading + (full_shape[-1] // (2 * pair_span), 2, pair_span))
    return jnp.flip(reshaped, axis=-2).reshape(full_shape)


def combine(matrices, current, partner, phase_row):
    blocks = matrices.astype(jnp.float32).reshape(2, N_BOX, R, R)
    own_term = jnp.einsum('dij,jdt->idt', blocks[0], current.astype(jnp.float32))
    partner_term = jnp.einsum('dij,jdt->idt', blocks[1], partner.astype(jnp.float32))
    return (jnp.cos(phase_row)[None] * own_term + jnp.sin(phase_row)[None] * partner_term).astype(jnp.bfloat16)


def reference(source_field, project_mats, local_mats, cross_mats, angles, evaluate_mats):
    field_cube = source_field.astype(jnp.float32).reshape(Q, N_BOX, BOX_DEV)
    projector = project_mats.astype(jnp.float32).reshape(N_BOX, R, Q)
    current = jnp.einsum('diq,qdt->idt', projector, field_cube).astype(jnp.bfloat16)
    phases = angles.astype(jnp.float32).reshape(LOCAL + LEVELS, N_BOX, BOX_DEV)
    local_bits = (BOX_DEV & -BOX_DEV).bit_length() - 1
    box_bits = N_BOX.bit_length() - 1
    for level_idx in range(LOCAL):
        pair_span = 1 << (level_idx % local_bits)
        partner = flip_last(current, pair_span)
        current = combine(local_mats[level_idx], current, partner, phases[level_idx])
    for level_idx in range(LEVELS):
        level_bit = (box_bits - 1 - level_idx) % box_bits
        flat = current.reshape(R, N_BOX * BOX_DEV)
        partner = flip_last(flat, BOX_DEV << level_bit).reshape(R, N_BOX, BOX_DEV)
        current = combine(cross_mats[level_idx], current, partner, phases[LOCAL + level_idx])
    group_size = BOX_DEV // N_BOX
    switched = current.reshape(R, N_BOX, N_BOX, group_size).transpose(0, 2, 1, 3).reshape(R, N_BOX, BOX_DEV)
    evaluator = evaluate_mats.astype(jnp.float32).reshape(N_BOX, Q, R)
    pixels_out = jnp.einsum('gqr,rgs->qgs', evaluator, switched.astype(jnp.float32))
    return pixels_out.reshape(Q, N_BOX * BOX_DEV).astype(jnp.bfloat16)
```

```python
import jax
import jax.numpy as jnp
from jax import lax
from jax.experimental import pallas as pl
from jax.experimental.pallas import tpu as pltpu
from jax.sharding import PartitionSpec as P

R = 64
TILE = 256
BF = jnp.bfloat16
F32 = jnp.float32

NX, NZ, NC = 4, 8, 2


def dot(a, b):
    return jnp.dot(a, b, preferred_element_type=F32)


def cos_sin(t):
    h = 0.5 * t
    q = h * h
    s = 1.0 + q * (
        -1.0 / 6 + q * (1.0 / 120 + q * (-1.0 / 5040 + q * (1.0 / 362880 + q * (-1.0 / 39916800 + q * (1.0 / 6227020800)))))
    )
    s = s * h
    c = 1.0 + q * (
        -0.5 + q * (1.0 / 24 + q * (-1.0 / 720 + q * (1.0 / 40320 + q * (-1.0 / 3628800 + q * (1.0 / 479001600)))))
    )
    return 1.0 - 2.0 * s * s, 2.0 * s * c


def mix(mat, own, partner, c, s):
    return dot(mat, jnp.concatenate([own * c, partner * s], axis=0)).astype(BF)


def row(values, i):
    return values[i : i + 1].astype(BF)


def local_kernel(block_ref, src_ref, ang_ref, proj_ref, mats_ref, out_ref):
    tiles = src_ref.shape[1] // TILE
    levels = mats_ref.shape[0]
    ang = ang_ref[...].astype(F32)
    cos, sin = cos_sin(ang[:levels])
    proj = proj_ref[...]
    x = [dot(proj, src_ref[:, i * TILE : (i + 1) * TILE]).astype(BF) for i in range(tiles)]
    to = lax.broadcasted_iota(jnp.int32, (TILE, TILE), 1)
    frm = lax.broadcasted_iota(jnp.int32, (TILE, TILE), 0)
    for level in range(levels):
        span = 1 << level
        if span == 128:
            xp = [jnp.concatenate([v[:, 128:], v[:, :128]], axis=1) for v in x]
        else:
            perm = jnp.where(frm == (to ^ span), 1.0, 0.0).astype(BF)
            every = dot(jnp.concatenate(x, axis=0), perm).astype(BF)
            xp = [every[i * R : (i + 1) * R] for i in range(tiles)]
        mat = jnp.concatenate([mats_ref[level, 0], mats_ref[level, 1]], axis=1)
        c, s = row(cos, level), row(sin, level)
        x = [
            mix(mat, x[i], xp[i], c[:, i * TILE : (i + 1) * TILE], s[:, i * TILE : (i + 1) * TILE])
            for i in range(tiles)
        ]
    for i in range(tiles):
        out_ref[0, i * R : (i + 1) * R] = x[i]
    a = jnp.concatenate(
        [ang[levels + 2 : levels + 6], ang[levels : levels + 2], jnp.zeros((2, ang.shape[1]), F32)], axis=0
    )
    a = jnp.concatenate([a[:, i * TILE : (i + 1) * TILE] for i in range(tiles)], axis=0)
    out_ref[0, tiles * R : tiles * R + tiles * 8] = a.astype(BF)


def local_levels(blocks, source_field, angles, project_mats, local_mats):
    n = blocks.shape[0]
    q, columns = source_field.shape
    width = columns // NX
    rows = NZ * R + NZ * 8
    return pl.pallas_call(
        local_kernel,
        grid_spec=pltpu.PrefetchScalarGridSpec(
            num_scalar_prefetch=1,
            grid=(n,),
            in_specs=[
                pl.BlockSpec((q, width), lambda i, b: (0, b[i])),
                pl.BlockSpec((angles.shape[0], width), lambda i, b: (0, b[i])),
                pl.BlockSpec(project_mats.shape, lambda i, b: (0, 0)),
                pl.BlockSpec(local_mats.shape, lambda i, b: (0, 0, 0, 0)),
            ],
            out_specs=pl.BlockSpec((1, rows, TILE), lambda i, b: (i, 0, 0)),
        ),
        out_shape=jax.ShapeDtypeStruct((n, rows, TILE), BF),
        compiler_params=pltpu.CompilerParams(vmem_limit_bytes=48 * 2**20),
    )(blocks, source_field, angles, project_mats, local_mats)


def x_kernel(*refs):
    data, angs, mats, out_ref = refs[:4], refs[4:8], refs[8:12], refs[12]
    tiles = data[0].shape[1] // R
    phases = [a[0].astype(F32) for a in angs]
    for i in range(tiles):
        x = [d[0, i * R : (i + 1) * R] for d in data]
        t = [angs_rows(p, i) for p in phases]
        cs = [cos_sin(v) for v in t]
        for level, bit in ((0, 2), (1, 1)):
            x = [
                mix(mats[j][level], x[j], x[j ^ bit], row(cs[j][0], 4 + level), row(cs[j][1], 4 + level))
                for j in range(4)
            ]
        for j in range(4):
            out_ref[i, j * R : (j + 1) * R] = x[j]
        out_ref[i, 4 * R :] = jnp.concatenate([v[:4] for v in t], axis=0).astype(BF)


def angs_rows(phases, i):
    return phases[i * 8 : (i + 1) * 8]


def x_levels(messages, mats):
    rows = 4 * R + 16
    specs = [pl.BlockSpec((1, NZ * R, TILE), lambda i: (0, 0, 0)) for _ in messages]
    ang_specs = [pl.BlockSpec((1, NZ * 8, TILE), lambda i: (0, 8, 0)) for _ in messages]
    mat_specs = [pl.BlockSpec((2, R, 2 * R), lambda i: (0, 0, 0)) for _ in mats]
    return pl.pallas_call(
        x_kernel,
        grid=(1,),
        in_specs=specs + ang_specs + mat_specs,
        out_specs=pl.BlockSpec((NZ, rows, TILE), lambda i: (0, 0, 0)),
        out_shape=jax.ShapeDtypeStruct((NZ, rows, TILE), BF),
        compiler_params=pltpu.CompilerParams(vmem_limit_bytes=48 * 2**20),
    )(*messages, *messages, *mats)


def z_kernel(core_ref, data_ref, ang_ref, mats_ref, keep_ref, send_ref):
    j = pl.program_id(0)
    low = core_ref[0] == 0
    x = [data_ref[k] for k in range(NZ)]
    cs = []
    for k in range(NZ):
        cs.append(cos_sin(ang_ref[k, pl.ds(0, 16)].astype(F32)))
    def pick(v):
        out = v[0:4]
        for n in range(1, 4):
            out = jnp.where(j == n, v[4 * n : 4 * n + 4], out)
        return out

    cs = [(pick(c), pick(s)) for c, s in cs]
    for level, bit in ((0, 4), (1, 2), (2, 1)):
        x = [
            mix(mats_ref[k, 0, level], x[k], x[k ^ bit], row(cs[k][0], level), row(cs[k][1], level))
            for k in range(NZ)
        ]
    for k in range(NZ):
        at = pl.ds(pl.multiple_of(j * (NZ * R) + k * R, R), R)
        lo, hi = x[k][:, :128], x[k][:, 128:]
        keep_ref[at] = jnp.where(low, lo, hi)
        send_ref[at] = jnp.where(low, hi, lo)

    @pl.when(j == 0)
    def _():
        for k in range(NZ):
            at = pl.ds(4 * NZ * R + k * 16, 16)
            a = ang_ref[k]
            lo, hi = a[:, :128], a[:, 128:]
            keep_ref[at] = jnp.where(low, lo, hi)
            send_ref[at] = jnp.where(low, hi, lo)


def z_levels(core, moved, mats):
    rows = 4 * NZ * R + NZ * 16
    out = jax.ShapeDtypeStruct((rows, 128), BF)
    return pl.pallas_call(
        z_kernel,
        grid_spec=pltpu.PrefetchScalarGridSpec(
            num_scalar_prefetch=1,
            grid=(4,),
            in_specs=[
                pl.BlockSpec((NZ, R, TILE), lambda j, c: (0, j, 0)),
                pl.BlockSpec((NZ, 16, TILE), lambda j, c: (0, 16, 0)),
                pl.BlockSpec((NZ, 1, 4, R, 2 * R), lambda j, c: (0, j, 0, 0, 0)),
            ],
            out_specs=[pl.BlockSpec((rows, 128), lambda j, c: (0, 0))] * 2,
        ),
        out_shape=[out, out],
        compiler_params=pltpu.CompilerParams(vmem_limit_bytes=48 * 2**20),
    )(core, moved, moved, mats)


def last_kernel(where_ref, own_ref, oth_ref, own_ang_ref, oth_ang_ref, own_mats_ref, oth_mats_ref, eval_ref, out_ref):
    j = pl.program_id(0)
    low = where_ref[4] == 0
    ev = eval_ref[...]

    def phases(ref, k):
        v = ref[pl.ds(k * 16, 16)].astype(F32)
        out = v[3:4]
        for n in range(1, 4):
            out = jnp.where(j == n, v[4 * n + 3 : 4 * n + 4], out)
        return out

    own_c, own_s = cos_sin(jnp.concatenate([phases(own_ang_ref, k) for k in range(NZ)], axis=0))
    oth_c, oth_s = cos_sin(jnp.concatenate([phases(oth_ang_ref, k) for k in range(NZ)], axis=0))
    for k in range(NZ):
        own = own_ref[k * R : (k + 1) * R]
        oth = oth_ref[k * R : (k + 1) * R]
        y_own = mix(own_mats_ref[k, 0, 0], own, oth, row(own_c, k), row(own_s, k))
        y_oth = mix(oth_mats_ref[k, 0], oth, own, row(oth_c, k), row(oth_s, k))
        y = jnp.concatenate([jnp.where(low, y_own, y_oth), jnp.where(low, y_oth, y_own)], axis=1)
        out_ref[:, k * TILE : (k + 1) * TILE] = dot(ev, y).astype(BF)


def last_level(where, keep, received, mats, other_mats, evaluate_mats):
    q = evaluate_mats.shape[0]
    columns = 64 * 128
    return pl.pallas_call(
        last_kernel,
        grid_spec=pltpu.PrefetchScalarGridSpec(
            num_scalar_prefetch=1,
            grid=(4,),
            in_specs=[
                pl.BlockSpec((NZ * R, 128), lambda j, w: (j, 0)),
                pl.BlockSpec((NZ * R, 128), lambda j, w: (j, 0)),
                pl.BlockSpec((NZ * 16, 128), lambda j, w: (16, 0)),
                pl.BlockSpec((NZ * 16, 128), lambda j, w: (16, 0)),
                pl.BlockSpec((NZ, 1, 1, R, 2 * R), lambda j, w: (0, j, 3, 0, 0)),
                pl.BlockSpec((NZ, 1, R, 2 * R), lambda j, w: (0, j, 0, 0)),
                pl.BlockSpec(evaluate_mats.shape, lambda j, w: (0, 0)),
            ],
            out_specs=pl.BlockSpec((q, columns // 4), lambda j, w: (0, w[j])),
        ),
        out_shape=jax.ShapeDtypeStruct((q, columns), BF),
        compiler_params=pltpu.CompilerParams(vmem_limit_bytes=48 * 2**20),
    )(where, keep, received, keep, received, mats, other_mats, evaluate_mats)


def shards(source_field, project_mats, local_mats, cross_mats, angles, evaluate_mats):
    box = lax.axis_index("box")
    x, core = box // (NZ * NC), box % NC
    count = NX * NZ * NC

    def along_x(values, j):
        return lax.ppermute(values, "box", [(i, i ^ (j * NZ * NC)) for i in range(count)])

    def across(values):
        return lax.ppermute(values, "box", [(i, i ^ 1) for i in range(count)])

    z_groups = [[xx * NZ * NC + z * NC + c for z in range(NZ)] for xx in range(NX) for c in range(NC)]

    own_mats = jnp.concatenate([cross_mats[:, 0], cross_mats[:, 1]], axis=-1)
    slot_mats = [own_mats] + [along_x(own_mats, j) for j in (1, 2, 3)]
    gathered = lax.all_gather(jnp.stack([m[2:] for m in slot_mats]), "box", axis=0, axis_index_groups=z_groups)

    def local(*slots):
        blocks = jnp.stack([x ^ j for j in slots]).astype(jnp.int32)
        return local_levels(blocks, source_field, angles, project_mats, local_mats)

    m2 = along_x(local(2), 2)
    m1 = along_x(local(1), 1)
    m3 = along_x(local(3), 3)
    m0 = local(0)
    sent = x_levels([m0, m1, m2, m3], slot_mats)
    moved = lax.all_to_all(sent, "box", 0, 0, tiled=True, axis_index_groups=z_groups)
    keep, send = z_levels(core[None].astype(jnp.int32), moved, gathered)
    other_mats = across(gathered[:, :, 3])
    received = across(send)
    where = jnp.stack([x, x ^ 1, x ^ 2, x ^ 3, core]).astype(jnp.int32)
    return last_level(where, keep, received, gathered, other_mats, evaluate_mats)


def solution(mesh):
    in_specs = (
        P("src", "box"),
        P("box", None),
        P(None, None, "box", None),
        P(None, None, "box", None),
        P(None, "box"),
        P("box", None),
    )
    out_specs = P("src", "box")
    return jax.shard_map(shards, mesh=mesh, in_specs=in_specs, out_specs=out_specs, check_vma=False)
```

```python
import functools

import jax
import jax.numpy as jnp
from jax import lax
from jax.experimental import pallas as pl
from jax.experimental.pallas import tpu as pltpu
from jax.sharding import PartitionSpec as P

R = 64
TILE = 256
BF = jnp.bfloat16
F32 = jnp.float32

NX, NZ, NC, PLANES = 4, 8, 2, 4
BLOCKS = NX * NZ
ROWS = 2 * R + 16
PARAMS = pltpu.CompilerParams(vmem_limit_bytes=60 * 2**20)
SLOTS = [(j, t, i) for j in range(NX) for t in range(PLANES) for i in range(2)]


def dot(a, b):
    return jnp.dot(a, b, preferred_element_type=F32)


def cos_sin(t):
    h = 0.5 * t
    q = h * h
    s = 1.0 + q * (
        -1.0 / 6 + q * (1.0 / 120 + q * (-1.0 / 5040 + q * (1.0 / 362880 + q * (-1.0 / 39916800 + q * (1.0 / 6227020800)))))
    )
    s = s * h
    c = 1.0 + q * (
        -0.5 + q * (1.0 / 24 + q * (-1.0 / 720 + q * (1.0 / 40320 + q * (-1.0 / 3628800 + q * (1.0 / 479001600)))))
    )
    return 1.0 - 2.0 * s * s, 2.0 * s * c


def mix(mat, own, partner, c, s):
    return dot(mat, jnp.concatenate([own * c, partner * s], axis=0)).astype(BF)


def row(values, i):
    return values[i : i + 1].astype(BF)


def local_kernel(start, src_any, ang_any, proj_any, mats_any, *refs):
    out_ref, src_all, ang_all, proj_ref, mats_ref, sems = refs[-6:]
    step, steps, width = pl.program_id(0), src_all.shape[0], src_all.shape[2]

    def loads(n):
        columns = pl.ds((start + n) * width, width)
        return (
            pltpu.make_async_copy(src_any.at[:, columns], src_all.at[n], sems.at[n, 0]),
            pltpu.make_async_copy(ang_any.at[:, columns], ang_all.at[n], sems.at[n, 1]),
        )

    shared = (
        pltpu.make_async_copy(proj_any, proj_ref, sems.at[steps, 0]),
        pltpu.make_async_copy(mats_any, mats_ref, sems.at[steps, 1]),
    )

    @pl.when(step == 0)
    def _():
        for copy in (shared[0], *loads(0), shared[1]):
            copy.start()
        for n in range(1, steps):
            for copy in loads(n):
                copy.start()
        for copy in shared:
            copy.wait()

    for n in range(steps):

        @pl.when(step == n)
        def _():
            for copy in loads(n):
                copy.wait()

    src_ref = src_all.at[step]
    tiles = width // TILE
    levels = mats_ref.shape[0]
    ang = ang_all[step].astype(F32)
    cos, sin = cos_sin(ang[:levels])
    proj = proj_ref[...]
    x = [dot(proj, src_ref[:, i * TILE : (i + 1) * TILE]).astype(BF) for i in range(tiles)]
    to = lax.broadcasted_iota(jnp.int32, (TILE, TILE), 1)
    frm = lax.broadcasted_iota(jnp.int32, (TILE, TILE), 0)
    for level in range(levels):
        span = 1 << level
        if span == 128:
            xp = [jnp.concatenate([v[:, 128:], v[:, :128]], axis=1) for v in x]
        else:
            perm = jnp.where(frm == (to ^ span), 1.0, 0.0).astype(BF)
            every = dot(jnp.concatenate(x, axis=0), perm).astype(BF)
            xp = [every[i * R : (i + 1) * R] for i in range(tiles)]
        mat = jnp.concatenate([mats_ref[level, 0], mats_ref[level, 1]], axis=1)
        c, s = row(cos, level), row(sin, level)
        x = [
            mix(mat, x[i], xp[i], c[:, i * TILE : (i + 1) * TILE], s[:, i * TILE : (i + 1) * TILE])
            for i in range(tiles)
        ]
    a = jnp.concatenate([ang[levels : levels + 6], jnp.zeros((2, ang.shape[1]), F32)], axis=0)
    for i in range(tiles):
        lo, mid, hi = i * TILE, i * TILE + 128, (i + 1) * TILE
        out_ref[i, :R] = x[i][:, :128]
        out_ref[i, R : 2 * R] = x[i][:, 128:]
        out_ref[i, 2 * R :] = jnp.concatenate([a[:, lo:mid], a[:, mid:hi]], axis=0).astype(BF)


def local_levels(steps, start, before, source_field, angles, project_mats, local_mats):
    q, columns = source_field.shape
    width = columns // 4
    tiles = width // TILE
    args = [source_field, angles, project_mats, local_mats]
    if before is not None:
        args.append(before)
    return pl.pallas_call(
        functools.partial(local_kernel, start),
        grid=(steps,),
        in_specs=[pl.BlockSpec(memory_space=pltpu.HBM)] * len(args),
        out_specs=pl.BlockSpec((tiles, ROWS, 128), lambda i: (start + i, 0, 0)),
        out_shape=jax.ShapeDtypeStruct((BLOCKS, ROWS, 128), BF),
        scratch_shapes=[
            pltpu.VMEM((steps, q, width), BF),
            pltpu.VMEM((steps, angles.shape[0], width), BF),
            pltpu.VMEM(project_mats.shape, BF),
            pltpu.VMEM(local_mats.shape, BF),
            pltpu.SemaphoreType.DMA((steps + 1, 2)),
        ],
        input_output_aliases={4: 0} if before is not None else {},
        compiler_params=PARAMS,
    )(*args)


def chip_kernel(at_ref, data_ref, q0_ref, q1_ref, q2lo_ref, q2hi_ref, q3_ref, keep_ref, send_ref, mats_ref, sems):
    early, late = pl.ds(0, 3), pl.ds(3, 3)
    pieces = [(t, part, ref.at[part]) for part in (early, late) for t, ref in ((0, q0_ref), (1, q1_ref), (3, q3_ref))]
    pieces += [(2, early, q2lo_ref), (2, late, q2hi_ref)]
    copies = [
        pltpu.make_async_copy(ref, mats_ref.at[t, part], sems.at[n]) for n, (t, part, ref) in enumerate(pieces)
    ]
    for copy in copies:
        copy.start()
    low = at_ref[0] == 0
    x, cs, last = {}, {}, {}
    for n, slot in enumerate(SLOTS):
        block = at_ref[1 + n]
        x[slot] = jnp.concatenate([data_ref[block, :R], data_ref[block, R : 2 * R]], axis=1)
        a = data_ref[block, 2 * R :].astype(F32)
        cs[slot] = cos_sin(jnp.concatenate([a[:8], a[8:]], axis=1))
        last[slot] = (a[:8], a[8:])
    for copy in copies:
        copy.wait()
    flips = ((2, 0, 0), (1, 0, 0), (0, 2, 0), (0, 1, 0), (0, 0, 1))
    for level, flip in enumerate(flips):
        x = {
            (j, t, i): mix(
                mats_ref[t, level, j, i],
                x[j, t, i],
                x[j ^ flip[0], t ^ flip[1], i ^ flip[2]],
                row(cs[j, t, i][0], level),
                row(cs[j, t, i][1], level),
            )
            for j, t, i in SLOTS
        }
    for n, slot in enumerate(SLOTS):
        at = n * R
        lo, hi = x[slot][:, :128], x[slot][:, 128:]
        keep_ref[at : at + R] = jnp.where(low, lo, hi)
        send_ref[at : at + R] = jnp.where(low, hi, lo)
    for n in range(0, BLOCKS, 2):
        at = BLOCKS * R + n * 8
        (lo0, hi0), (lo1, hi1) = last[SLOTS[n]], last[SLOTS[n + 1]]
        lo, hi = jnp.concatenate([lo0, lo1], axis=0), jnp.concatenate([hi0, hi1], axis=0)
        keep_ref[at : at + 16] = jnp.where(low, lo, hi).astype(BF)
        send_ref[at : at + 16] = jnp.where(low, hi, lo).astype(BF)
    for n, (j, t, i) in enumerate(SLOTS):
        at = BLOCKS * (R + 8) + n * R
        keep_ref[at : at + R] = mats_ref[t, 5, j, i]
        send_ref[at : at + R] = mats_ref[t, 5, j, i]


def chip_levels(at, moved, mats):
    out = jax.ShapeDtypeStruct((BLOCKS * (2 * R + 8), 128), BF)
    vmem = pl.BlockSpec(memory_space=pltpu.VMEM)
    return pl.pallas_call(
        chip_kernel,
        in_specs=[pl.BlockSpec(memory_space=pltpu.SMEM), vmem] + [pl.BlockSpec(memory_space=pltpu.HBM)] * 5,
        out_specs=[vmem, vmem],
        out_shape=[out, out],
        scratch_shapes=[pltpu.VMEM((PLANES, 6, NX, 2, R, 2 * R), BF), pltpu.SemaphoreType.DMA((8,))],
        compiler_params=PARAMS,
    )(at, moved, *mats)


def last_kernel(at_ref, own_ref, oth_ref, eval_ref, out_ref):
    low = at_ref[0] == 0
    ev = eval_ref[...]
    for n in range(BLOCKS):
        if n % 2 == 0:
            a = BLOCKS * R + n * 8
            own_c, own_s = cos_sin(own_ref[a : a + 16].astype(F32))
            oth_c, oth_s = cos_sin(oth_ref[a : a + 16].astype(F32))
        at, r, m = n * R, 5 + 8 * (n % 2), BLOCKS * (R + 8) + n * R
        own, oth = own_ref[at : at + R], oth_ref[at : at + R]
        y_own = mix(own_ref[m : m + R], own, oth, row(own_c, r), row(own_s, r))
        y_oth = mix(oth_ref[m : m + R], oth, own, row(oth_c, r), row(oth_s, r))
        y = jnp.concatenate([jnp.where(low, y_own, y_oth), jnp.where(low, y_oth, y_own)], axis=1)
        column = pl.multiple_of(at_ref[1 + n] * TILE, TILE)
        out_ref[:, pl.ds(column, TILE)] = dot(ev, y).astype(BF)


def last_level(at, keep, received, evaluate_mats):
    vmem = pl.BlockSpec(memory_space=pltpu.VMEM)
    return pl.pallas_call(
        last_kernel,
        in_specs=[pl.BlockSpec(memory_space=pltpu.SMEM)] + [vmem] * 3,
        out_specs=vmem,
        out_shape=jax.ShapeDtypeStruct((evaluate_mats.shape[0], 64 * 128), BF),
        compiler_params=PARAMS,
    )(at, keep, received, evaluate_mats)


def shards(source_field, project_mats, local_mats, cross_mats, angles, evaluate_mats):
    box, plane = lax.axis_index("box"), lax.axis_index("src")
    x, z, core = box // (NZ * NC), box // NC % NZ, box % NC
    count = NX * NZ * NC

    def swap(values, distance):
        return lax.ppermute(values, "box", [(i, i ^ distance) for i in range(count)])

    def along_z(values, n):
        pairs = [
            (i * PLANES + p, (i ^ ((2 * p + n) * NC)) * PLANES + p) for i in range(count) for p in range(PLANES)
        ]
        return lax.ppermute(values, ("box", "src"), pairs)

    def along_src(values, t):
        return lax.ppermute(values, "src", [(p, p ^ t) for p in range(PLANES)])

    def after(value, *first):
        return lax.optimization_barrier((value, *first))[0]

    chips = [[xx * NZ * NC + zz * NC + c for xx in range(NX) for zz in range(NZ)] for c in range(NC)]

    own = jnp.concatenate([cross_mats[:, 0], cross_mats[:, 1]], axis=-1)
    pair = [along_z(own, n) for n in (0, 1)]
    first = local_levels(1, 0, None, source_field, angles, project_mats, local_mats)
    pair = jnp.stack([after(pair[0], first), pair[1]], axis=1)
    quarter = [pair] + [swap(pair, j * NZ * NC) for j in (1, 2, 3)]
    sent = local_levels(3, 1, after(first, pair), source_field, angles, project_mats, local_mats)
    sent, *quarter = lax.optimization_barrier((sent, *quarter))
    moved = lax.all_to_all(sent, "box", 0, 0, tiled=True, axis_index_groups=chips)
    quarter = jnp.stack(quarter, axis=1)
    q1, q3 = along_src(quarter, 1), along_src(quarter, 3)
    mats = [quarter, q1, along_src(q3[:3], 1), along_src(q1[3:], 3), q3]

    blocks = [(x ^ j) * NZ + (z ^ (((plane ^ t) << 1) | i)) for j, t, i in SLOTS]
    at = jnp.stack([core] + blocks).astype(jnp.int32)
    keep, send = chip_levels(at, moved, mats)
    received = swap(send, 1)
    return last_level(at, keep, received, evaluate_mats)


def solution(mesh):
    in_specs = (
        P("src", "box"),
        P("box", None),
        P(None, None, "box", None),
        P(None, None, "box", None),
        P(None, "box"),
        P("box", None),
    )
    out_specs = P("src", "box")
    return jax.shard_map(shards, mesh=mesh, in_specs=in_specs, out_specs=out_specs, check_vma=False)
```

```python
import functools

import jax
import jax.numpy as jnp
from jax import lax
from jax.experimental import pallas as pl
from jax.experimental.pallas import tpu as pltpu
from jax.sharding import PartitionSpec as P

R = 64
TILE = 256
BF = jnp.bfloat16
F32 = jnp.float32

NX, NZ, NC, PLANES = 4, 8, 2, 4
BLOCKS = NX * NZ
ROWS = 2 * R + 16
PARAMS = pltpu.CompilerParams(vmem_limit_bytes=60 * 2**20)
SMALL = pltpu.CompilerParams(vmem_limit_bytes=24 * 2**20)
SLOTS = [(j, t, i) for j in range(NX) for t in range(PLANES) for i in range(2)]


def place():
    box = lax.axis_index("box")
    return box // (NZ * NC), box // NC % NZ, box % NC, lax.axis_index("src")


def block_of(slot):
    x, z, _, plane = place()
    j, t, i = slot
    return (x ^ j) * NZ + (z ^ (((plane ^ t) << 1) | i))


def dot(a, b):
    return jnp.dot(a, b, preferred_element_type=F32)


def cos_sin(t):
    h = 0.5 * t
    q = h * h
    s = 1.0 + q * (
        -1.0 / 6 + q * (1.0 / 120 + q * (-1.0 / 5040 + q * (1.0 / 362880 + q * (-1.0 / 39916800 + q * (1.0 / 6227020800)))))
    )
    s = s * h
    c = 1.0 + q * (
        -0.5 + q * (1.0 / 24 + q * (-1.0 / 720 + q * (1.0 / 40320 + q * (-1.0 / 3628800 + q * (1.0 / 479001600)))))
    )
    return 1.0 - 2.0 * s * s, 2.0 * s * c


def mix(mat, own, partner, c, s):
    return dot(mat, jnp.concatenate([own * c, partner * s], axis=0)).astype(BF)


def row(values, i):
    return values[i : i + 1].astype(BF)


def local_kernel(start, src_any, ang_any, proj_any, mats_any, *refs):
    out_ref, src_all, ang_all, proj_ref, mats_ref, sems = refs[-6:]
    step, steps, width = pl.program_id(0), src_all.shape[0], src_all.shape[2]

    def loads(n):
        columns = pl.ds((start + n) * width, width)
        return (
            pltpu.make_async_copy(src_any.at[:, columns], src_all.at[n], sems.at[n, 0]),
            pltpu.make_async_copy(ang_any.at[:, columns], ang_all.at[n], sems.at[n, 1]),
        )

    shared = (
        pltpu.make_async_copy(proj_any, proj_ref, sems.at[steps, 0]),
        pltpu.make_async_copy(mats_any, mats_ref, sems.at[steps, 1]),
    )

    @pl.when(step == 0)
    def _():
        for copy in (shared[0], *loads(0), shared[1]):
            copy.start()
        for n in range(1, steps):
            for copy in loads(n):
                copy.start()
        for copy in shared:
            copy.wait()

    for n in range(steps):

        @pl.when(step == n)
        def _():
            for copy in loads(n):
                copy.wait()

    src_ref = src_all.at[step]
    tiles = width // TILE
    levels = mats_ref.shape[0]
    ang = ang_all[step].astype(F32)
    cos, sin = cos_sin(ang[:levels])
    proj = proj_ref[...]
    x = [dot(proj, src_ref[:, i * TILE : (i + 1) * TILE]).astype(BF) for i in range(tiles)]
    to = lax.broadcasted_iota(jnp.int32, (TILE, TILE), 1)
    frm = lax.broadcasted_iota(jnp.int32, (TILE, TILE), 0)
    for level in range(levels):
        span = 1 << level
        if span == 128:
            xp = [jnp.concatenate([v[:, 128:], v[:, :128]], axis=1) for v in x]
        else:
            perm = jnp.where(frm == (to ^ span), 1.0, 0.0).astype(BF)
            every = dot(jnp.concatenate(x, axis=0), perm).astype(BF)
            xp = [every[i * R : (i + 1) * R] for i in range(tiles)]
        mat = jnp.concatenate([mats_ref[level, 0], mats_ref[level, 1]], axis=1)
        c, s = row(cos, level), row(sin, level)
        x = [
            mix(mat, x[i], xp[i], c[:, i * TILE : (i + 1) * TILE], s[:, i * TILE : (i + 1) * TILE])
            for i in range(tiles)
        ]
    a = jnp.concatenate([ang[levels : levels + 6], jnp.zeros((2, ang.shape[1]), F32)], axis=0)
    for i in range(tiles):
        lo, mid, hi = i * TILE, i * TILE + 128, (i + 1) * TILE
        out_ref[i, :R] = x[i][:, :128]
        out_ref[i, R : 2 * R] = x[i][:, 128:]
        out_ref[i, 2 * R :] = jnp.concatenate([a[:, lo:mid], a[:, mid:hi]], axis=0).astype(BF)


def local_levels(steps, start, before, source_field, angles, project_mats, local_mats):
    q, columns = source_field.shape
    width = columns // 4
    tiles = width // TILE
    args = [source_field, angles, project_mats, local_mats]
    if before is not None:
        args.append(before)
    return pl.pallas_call(
        functools.partial(local_kernel, start),
        grid=(steps,),
        in_specs=[pl.BlockSpec(memory_space=pltpu.HBM)] * len(args),
        out_specs=pl.BlockSpec((tiles, ROWS, 128), lambda i: (start + i, 0, 0)),
        out_shape=jax.ShapeDtypeStruct((BLOCKS, ROWS, 128), BF),
        scratch_shapes=[
            pltpu.VMEM((steps, q, width), BF),
            pltpu.VMEM((steps, angles.shape[0], width), BF),
            pltpu.VMEM(project_mats.shape, BF),
            pltpu.VMEM(local_mats.shape, BF),
            pltpu.SemaphoreType.DMA((steps + 1, 2)),
        ],
        input_output_aliases={4: 0} if before is not None else {},
        compiler_params=PARAMS,
    )(*args)


def chip_kernel(data_ref, *refs):
    keep_ref, send_ref, mats_ref, sems = refs[-4:]
    copies = [
        [
            pltpu.make_async_copy(refs[p * PLANES + t], mats_ref.at[t, p], sems.at[p, t])
            for t in range(PLANES)
        ]
        for p in range(2)
    ]
    for copy in copies[0] + copies[1]:
        copy.start()
    low = place()[2] == 0
    x, cs, last = {}, {}, {}
    for slot in SLOTS:
        block = block_of(slot)
        x[slot] = jnp.concatenate([data_ref[block, :R], data_ref[block, R : 2 * R]], axis=1)
        a = data_ref[block, 2 * R :].astype(F32)
        cs[slot] = cos_sin(jnp.concatenate([a[:8], a[8:]], axis=1))
        last[slot] = (a[:8], a[8:])
    flips = ((2, 0, 0), (1, 0, 0), (0, 2, 0), (0, 1, 0), (0, 0, 1))
    for level, flip in enumerate(flips):
        if level % 3 == 0:
            for copy in copies[level // 3]:
                copy.wait()
        x = {
            (j, t, i): mix(
                mats_ref[t, level // 3, j, level % 3, i],
                x[j, t, i],
                x[j ^ flip[0], t ^ flip[1], i ^ flip[2]],
                row(cs[j, t, i][0], level),
                row(cs[j, t, i][1], level),
            )
            for j, t, i in SLOTS
        }
    for n, slot in enumerate(SLOTS):
        at = n * R
        lo, hi = x[slot][:, :128], x[slot][:, 128:]
        keep_ref[at : at + R] = jnp.where(low, lo, hi)
        send_ref[at : at + R] = jnp.where(low, hi, lo)
    for n in range(0, BLOCKS, 2):
        at = BLOCKS * R + n * 8
        (lo0, hi0), (lo1, hi1) = last[SLOTS[n]], last[SLOTS[n + 1]]
        lo, hi = jnp.concatenate([lo0, lo1], axis=0), jnp.concatenate([hi0, hi1], axis=0)
        keep_ref[at : at + 16] = jnp.where(low, lo, hi).astype(BF)
        send_ref[at : at + 16] = jnp.where(low, hi, lo).astype(BF)
    for n, (j, t, i) in enumerate(SLOTS):
        at = BLOCKS * (R + 8) + n * R
        keep_ref[at : at + R] = mats_ref[t, 1, j, 2, i]
        send_ref[at : at + R] = mats_ref[t, 1, j, 2, i]


def chip_levels(moved, early, late):
    out = jax.ShapeDtypeStruct((BLOCKS * (2 * R + 8), 128), BF)
    vmem = pl.BlockSpec(memory_space=pltpu.VMEM)
    return pl.pallas_call(
        chip_kernel,
        in_specs=[vmem] + [pl.BlockSpec(memory_space=pl.ANY)] * 8,
        out_specs=[vmem, vmem],
        out_shape=[out, out],
        scratch_shapes=[pltpu.VMEM((PLANES, 2, NX, 3, 2, R, 2 * R), BF), pltpu.SemaphoreType.DMA((2, PLANES))],
        compiler_params=SMALL,
    )(moved, *early, *late)


def last_kernel(own_ref, oth_ref, eval_ref, out_ref):
    low = place()[2] == 0
    ev = eval_ref[...]
    for n in range(BLOCKS):
        if n % 2 == 0:
            a = BLOCKS * R + n * 8
            own_c, own_s = cos_sin(own_ref[a : a + 16].astype(F32))
            oth_c, oth_s = cos_sin(oth_ref[a : a + 16].astype(F32))
        at, r, m = n * R, 5 + 8 * (n % 2), BLOCKS * (R + 8) + n * R
        own, oth = own_ref[at : at + R], oth_ref[at : at + R]
        y_own = mix(own_ref[m : m + R], own, oth, row(own_c, r), row(own_s, r))
        y_oth = mix(oth_ref[m : m + R], oth, own, row(oth_c, r), row(oth_s, r))
        y = jnp.concatenate([jnp.where(low, y_own, y_oth), jnp.where(low, y_oth, y_own)], axis=1)
        column = pl.multiple_of(block_of(SLOTS[n]) * TILE, TILE)
        out_ref[:, pl.ds(column, TILE)] = lax.dot_general(
            ev, y, (((0,), (0,)), ((), ())), preferred_element_type=F32
        ).astype(BF)


def last_level(keep, received, evaluate_mats):
    vmem = pl.BlockSpec(memory_space=pltpu.VMEM)
    return pl.pallas_call(
        last_kernel,
        in_specs=[vmem] * 3,
        out_specs=vmem,
        out_shape=jax.ShapeDtypeStruct((evaluate_mats.shape[1], 64 * 128), BF),
        compiler_params=SMALL,
    )(keep, received, evaluate_mats)


def shards(source_field, project_mats, local_mats, cross_mats, angles, evaluate_mats):
    count = NX * NZ * NC

    def swap(values, distance):
        return lax.ppermute(values, "box", [(i, i ^ distance) for i in range(count)])

    def to_plane(values):
        pairs = [(i * PLANES + p, (i ^ (2 * p * NC)) * PLANES + p) for i in range(count) for p in range(PLANES)]
        return lax.ppermute(values, ("box", "src"), pairs)

    def along_src(values, t):
        return lax.ppermute(values, "src", [(p, p ^ t) for p in range(PLANES)])

    def after(value, *first):
        return lax.optimization_barrier((value, *first))[0]

    chips = [[xx * NZ * NC + zz * NC + c for xx in range(NX) for zz in range(NZ)] for c in range(NC)]

    own = jnp.concatenate([cross_mats[:, 0], cross_mats[:, 1]], axis=-1)
    far = to_plane(own)
    first = local_levels(1, 0, None, source_field, angles, project_mats, local_mats)
    far = after(far, first)
    pair = jnp.stack([far, swap(far, NC)], axis=1)
    quarter = [pair] + [swap(pair, j * NZ * NC) for j in (1, 2, 3)]
    sent = local_levels(3, 1, after(first, pair), source_field, angles, project_mats, local_mats)
    sent, *quarter = lax.optimization_barrier((sent, *quarter))
    moved = lax.all_to_all(sent, "box", 0, 0, tiled=True, axis_index_groups=chips)
    early, late = (jnp.stack([q[p : p + 3] for q in quarter]) for p in (0, 3))
    early3, late1 = along_src(early, 3), along_src(late, 1)
    early1, late3 = along_src(early, 1), along_src(late, 3)
    early2, late2 = along_src(early3, 1), along_src(late1, 3)

    keep, send = chip_levels(moved, (early, early1, early2, early3), (late, late1, late2, late3))
    received = swap(send, 1)
    return last_level(keep, received, evaluate_mats.T)


def solution(mesh):
    in_specs = (
        P("src", "box"),
        P("box", None),
        P(None, None, "box", None),
        P(None, None, "box", None),
        P(None, "box"),
        P("box", None),
    )
    out_specs = P("src", "box")
    return jax.shard_map(shards, mesh=mesh, in_specs=in_specs, out_specs=out_specs, check_vma=False)
```

```python
import functools

import jax
import jax.numpy as jnp
from jax import lax
from jax.experimental import pallas as pl
from jax.experimental.pallas import tpu as pltpu
from jax.sharding import PartitionSpec as P

R = 64
TILE = 256
BF = jnp.bfloat16
F32 = jnp.float32

NX, NZ, NC, PLANES = 4, 8, 2, 4
BLOCKS = NX * NZ
ROWS = 2 * R + 16
PARAMS = pltpu.CompilerParams(vmem_limit_bytes=60 * 2**20)
SMALL = pltpu.CompilerParams(vmem_limit_bytes=24 * 2**20)
SLOTS = [(j, t, i) for j in range(NX) for t in range(PLANES) for i in range(2)]


def place():
    box = lax.axis_index("box")
    return box // (NZ * NC), box // NC % NZ, box % NC, lax.axis_index("src")


def block_of(slot):
    x, z, _, plane = place()
    j, t, i = slot
    return (x ^ j) * NZ + (z ^ (((plane ^ t) << 1) | i))


def dot(a, b):
    return jnp.dot(a, b, preferred_element_type=F32)


def cos_sin(t):
    h = 0.5 * t
    q = h * h
    s = 1.0 + q * (
        -1.0 / 6 + q * (1.0 / 120 + q * (-1.0 / 5040 + q * (1.0 / 362880 + q * (-1.0 / 39916800 + q * (1.0 / 6227020800)))))
    )
    s = s * h
    c = 1.0 + q * (
        -0.5 + q * (1.0 / 24 + q * (-1.0 / 720 + q * (1.0 / 40320 + q * (-1.0 / 3628800 + q * (1.0 / 479001600)))))
    )
    return 1.0 - 2.0 * s * s, 2.0 * s * c


def mix(mat, own, partner, c, s):
    return dot(mat, jnp.concatenate([own * c, partner * s], axis=0)).astype(BF)


def row(values, i):
    return values[i : i + 1].astype(BF)


def local_kernel(start, src_any, ang_any, proj_any, mats_any, *refs):
    out_ref, src_all, ang_all, proj_ref, mats_ref, sems = refs[-6:]
    step, steps, width = pl.program_id(0), src_all.shape[0], src_all.shape[2]

    def loads(n):
        columns = pl.ds((start + n) * width, width)
        return (
            pltpu.make_async_copy(src_any.at[:, columns], src_all.at[n], sems.at[n, 0]),
            pltpu.make_async_copy(ang_any.at[:, columns], ang_all.at[n], sems.at[n, 1]),
        )

    shared = (
        pltpu.make_async_copy(proj_any, proj_ref, sems.at[steps, 0]),
        pltpu.make_async_copy(mats_any, mats_ref, sems.at[steps, 1]),
    )

    @pl.when(step == 0)
    def _():
        for copy in (shared[0], *loads(0), shared[1]):
            copy.start()
        for n in range(1, steps):
            for copy in loads(n):
                copy.start()
        for copy in shared:
            copy.wait()

    for n in range(steps):

        @pl.when(step == n)
        def _():
            for copy in loads(n):
                copy.wait()

    src_ref = src_all.at[step]
    tiles = width // TILE
    levels = mats_ref.shape[0]
    ang = ang_all[step].astype(F32)
    cos, sin = cos_sin(ang[:levels])
    proj = proj_ref[...]
    x = [dot(proj, src_ref[:, i * TILE : (i + 1) * TILE]).astype(BF) for i in range(tiles)]
    to = lax.broadcasted_iota(jnp.int32, (TILE, TILE), 1)
    frm = lax.broadcasted_iota(jnp.int32, (TILE, TILE), 0)
    for level in range(levels):
        span = 1 << level
        if span == 128:
            xp = [jnp.concatenate([v[:, 128:], v[:, :128]], axis=1) for v in x]
        else:
            perm = jnp.where(frm == (to ^ span), 1.0, 0.0).astype(BF)
            every = dot(jnp.concatenate(x, axis=0), perm).astype(BF)
            xp = [every[i * R : (i + 1) * R] for i in range(tiles)]
        mat = jnp.concatenate([mats_ref[level, 0], mats_ref[level, 1]], axis=1)
        c, s = row(cos, level), row(sin, level)
        x = [
            mix(mat, x[i], xp[i], c[:, i * TILE : (i + 1) * TILE], s[:, i * TILE : (i + 1) * TILE])
            for i in range(tiles)
        ]
    a = jnp.concatenate([ang[levels : levels + 6], jnp.zeros((2, ang.shape[1]), F32)], axis=0)
    for i in range(tiles):
        lo, mid, hi = i * TILE, i * TILE + 128, (i + 1) * TILE
        out_ref[i, :R] = x[i][:, :128]
        out_ref[i, R : 2 * R] = x[i][:, 128:]
        out_ref[i, 2 * R :] = jnp.concatenate([a[:, lo:mid], a[:, mid:hi]], axis=0).astype(BF)


def local_levels(steps, parts, start, before, source_field, angles, project_mats, local_mats):
    q, columns = source_field.shape
    width = columns // parts
    tiles = width // TILE
    args = [source_field, angles, project_mats, local_mats]
    if before is not None:
        args.append(before)
    return pl.pallas_call(
        functools.partial(local_kernel, start),
        grid=(steps,),
        in_specs=[pl.BlockSpec(memory_space=pltpu.HBM)] * len(args),
        out_specs=pl.BlockSpec((tiles, ROWS, 128), lambda i: (start + i, 0, 0)),
        out_shape=jax.ShapeDtypeStruct((BLOCKS, ROWS, 128), BF),
        scratch_shapes=[
            pltpu.VMEM((steps, q, width), BF),
            pltpu.VMEM((steps, angles.shape[0], width), BF),
            pltpu.VMEM(project_mats.shape, BF),
            pltpu.VMEM(local_mats.shape, BF),
            pltpu.SemaphoreType.DMA((steps + 1, 2)),
        ],
        input_output_aliases={4: 0} if before is not None else {},
        compiler_params=PARAMS,
    )(*args)


def phases_kernel(ang_ref, cos_ref, sin_ref):
    cos_ref[...], sin_ref[...] = cos_sin(ang_ref[...].astype(F32))


def phases(moved):
    out = jax.ShapeDtypeStruct((BLOCKS, 16, 128), F32)
    spec = pl.BlockSpec((BLOCKS, 16, 128), lambda i: (0, 0, 0))
    return pl.pallas_call(
        phases_kernel,
        grid=(1,),
        in_specs=[pl.BlockSpec((BLOCKS, 16, 128), lambda i: (0, 2 * R // 16, 0))],
        out_specs=[spec, spec],
        out_shape=[out, out],
        compiler_params=SMALL,
    )(moved)


def chip_kernel(data_ref, cos_ref, sin_ref, *refs):
    keep_ref, send_ref = refs[-2:]
    low = place()[2] == 0
    x, cs, last = {}, {}, {}
    for slot in SLOTS:
        block = block_of(slot)
        x[slot] = jnp.concatenate([data_ref[block, :R], data_ref[block, R : 2 * R]], axis=1)
        c, s = cos_ref[block], sin_ref[block]
        cs[slot] = (jnp.concatenate([c[:8], c[8:]], axis=1), jnp.concatenate([s[:8], s[8:]], axis=1))
        a = data_ref[block, 2 * R :].astype(F32)
        last[slot] = (a[:8], a[8:])
    flips = ((2, 0, 0), (1, 0, 0), (0, 2, 0), (0, 1, 0), (0, 0, 1))
    for level, flip in enumerate(flips):
        x = {
            (j, t, i): mix(
                refs[level // 3 * PLANES + t][j, level % 3, i],
                x[j, t, i],
                x[j ^ flip[0], t ^ flip[1], i ^ flip[2]],
                row(cs[j, t, i][0], level),
                row(cs[j, t, i][1], level),
            )
            for j, t, i in SLOTS
        }
    for n, slot in enumerate(SLOTS):
        at = n * R
        lo, hi = x[slot][:, :128], x[slot][:, 128:]
        keep_ref[at : at + R] = jnp.where(low, lo, hi)
        send_ref[at : at + R] = jnp.where(low, hi, lo)
    for n in range(0, BLOCKS, 2):
        at = BLOCKS * R + n * 8
        (lo0, hi0), (lo1, hi1) = last[SLOTS[n]], last[SLOTS[n + 1]]
        lo, hi = jnp.concatenate([lo0, lo1], axis=0), jnp.concatenate([hi0, hi1], axis=0)
        keep_ref[at : at + 16] = jnp.where(low, lo, hi).astype(BF)
        send_ref[at : at + 16] = jnp.where(low, hi, lo).astype(BF)
    for n, (j, t, i) in enumerate(SLOTS):
        at = BLOCKS * (R + 8) + n * R
        keep_ref[at : at + R] = refs[PLANES + t][j, 2, i]
        send_ref[at : at + R] = refs[PLANES + t][j, 2, i]


def chip_levels(moved, cos, sin, early, late):
    out = jax.ShapeDtypeStruct((BLOCKS * (2 * R + 8), 128), BF)
    vmem = pl.BlockSpec(memory_space=pltpu.VMEM)
    return pl.pallas_call(
        chip_kernel,
        in_specs=[vmem] * 11,
        out_specs=[vmem, vmem],
        out_shape=[out, out],
        compiler_params=SMALL,
    )(moved, cos, sin, *early, *late)


def last_kernel(own_ref, oth_ref, eval_ref, out_ref):
    low = place()[2] == 0
    ev = eval_ref[...]
    for n in range(BLOCKS):
        if n % 2 == 0:
            a = BLOCKS * R + n * 8
            own_c, own_s = cos_sin(own_ref[a : a + 16].astype(F32))
            oth_c, oth_s = cos_sin(oth_ref[a : a + 16].astype(F32))
        at, r, m = n * R, 5 + 8 * (n % 2), BLOCKS * (R + 8) + n * R
        own, oth = own_ref[at : at + R], oth_ref[at : at + R]
        y_own = mix(own_ref[m : m + R], own, oth, row(own_c, r), row(own_s, r))
        y_oth = mix(oth_ref[m : m + R], oth, own, row(oth_c, r), row(oth_s, r))
        y = jnp.concatenate([jnp.where(low, y_own, y_oth), jnp.where(low, y_oth, y_own)], axis=1)
        column = pl.multiple_of(block_of(SLOTS[n]) * TILE, TILE)
        out_ref[:, pl.ds(column, TILE)] = lax.dot_general(
            ev, y, (((0,), (0,)), ((), ())), preferred_element_type=F32
        ).astype(BF)


def last_level(keep, received, evaluate_mats):
    vmem = pl.BlockSpec(memory_space=pltpu.VMEM)
    return pl.pallas_call(
        last_kernel,
        in_specs=[vmem] * 3,
        out_specs=vmem,
        out_shape=jax.ShapeDtypeStruct((evaluate_mats.shape[1], 64 * 128), BF),
        compiler_params=SMALL,
    )(keep, received, evaluate_mats)


def shards(source_field, project_mats, local_mats, cross_mats, angles, evaluate_mats):
    count = NX * NZ * NC

    def swap(values, distance):
        return lax.ppermute(values, "box", [(i, i ^ distance) for i in range(count)])

    def to_plane(values):
        pairs = [(i * PLANES + p, (i ^ (2 * p * NC)) * PLANES + p) for i in range(count) for p in range(PLANES)]
        return lax.ppermute(values, ("box", "src"), pairs)

    def along_src(values, t):
        return lax.ppermute(values, "src", [(p, p ^ t) for p in range(PLANES)])

    def after(value, *first):
        return lax.optimization_barrier((value, *first))[0]

    chips = [[xx * NZ * NC + zz * NC + c for xx in range(NX) for zz in range(NZ)] for c in range(NC)]

    own = jnp.concatenate([cross_mats[:, 0], cross_mats[:, 1]], axis=-1)
    far = to_plane(own)
    first = local_levels(1, 2, 0, None, source_field, angles, project_mats, local_mats)
    far = after(far, first)
    pair = jnp.stack([far, swap(far, NC)], axis=1)
    quarter = [pair] + [swap(pair, j * NZ * NC) for j in (1, 2, 3)]
    sent = local_levels(1, 2, 1, after(first, pair), source_field, angles, project_mats, local_mats)
    sent, *quarter = lax.optimization_barrier((sent, *quarter))
    moved = lax.all_to_all(sent, "box", 0, 0, tiled=True, axis_index_groups=chips)
    early, late = (jnp.stack([q[p : p + 3] for q in quarter]) for p in (0, 3))
    early3, late1 = along_src(early, 3), along_src(late, 1)
    early1, late3 = along_src(early, 1), along_src(late, 3)
    early2, late2 = along_src(early3, 1), along_src(late1, 3)

    keep, send = chip_levels(moved, *phases(moved), (early, early1, early2, early3), (late, late1, late2, late3))
    received = swap(send, 1)
    return last_level(keep, received, evaluate_mats.T)


def solution(mesh):
    in_specs = (
        P("src", "box"),
        P("box", None),
        P(None, None, "box", None),
        P(None, None, "box", None),
        P(None, "box"),
        P("box", None),
    )
    out_specs = P("src", "box")
    return jax.shard_map(shards, mesh=mesh, in_specs=in_specs, out_specs=out_specs, check_vma=False)
```

```python
import functools

import jax
import jax.numpy as jnp
from jax import lax
from jax.experimental import pallas as pl
from jax.experimental.pallas import tpu as pltpu
from jax.sharding import PartitionSpec as P

R = 64
TILE = 256
BF = jnp.bfloat16
F32 = jnp.float32

NX, NZ, NC, PLANES = 4, 8, 2, 4
BLOCKS = NX * NZ
ROWS = 2 * R + 16
PARAMS = pltpu.CompilerParams(vmem_limit_bytes=60 * 2**20)
SMALL = pltpu.CompilerParams(vmem_limit_bytes=24 * 2**20)
SLOTS = [(j, t, i) for j in range(NX) for t in range(PLANES) for i in range(2)]


def place():
    box = lax.axis_index("box")
    return box // (NZ * NC), box // NC % NZ, box % NC, lax.axis_index("src")


def block_of(slot):
    x, z, _, plane = place()
    j, t, i = slot
    return (x ^ j) * NZ + (z ^ (((plane ^ t) << 1) | i))


def dot(a, b):
    return jnp.dot(a, b, preferred_element_type=F32)


def cos_sin(t):
    h = 0.5 * t
    q = h * h
    s = 1.0 + q * (
        -1.0 / 6 + q * (1.0 / 120 + q * (-1.0 / 5040 + q * (1.0 / 362880 + q * (-1.0 / 39916800 + q * (1.0 / 6227020800)))))
    )
    s = s * h
    c = 1.0 + q * (
        -0.5 + q * (1.0 / 24 + q * (-1.0 / 720 + q * (1.0 / 40320 + q * (-1.0 / 3628800 + q * (1.0 / 479001600)))))
    )
    return 1.0 - 2.0 * s * s, 2.0 * s * c


def mix(mat, own, partner, c, s):
    return dot(mat, jnp.concatenate([own * c, partner * s], axis=0)).astype(BF)


def row(values, i):
    return values[i : i + 1].astype(BF)


def local_kernel(start, src_any, ang_any, proj_any, mats_any, *refs):
    out_ref, src_all, ang_all, proj_ref, mats_ref, sems = refs[-6:]
    step, steps, width = pl.program_id(0), src_all.shape[0], src_all.shape[2]

    def loads(n):
        columns = pl.ds((start + n) * width, width)
        return (
            pltpu.make_async_copy(src_any.at[:, columns], src_all.at[n], sems.at[n, 0]),
            pltpu.make_async_copy(ang_any.at[:, columns], ang_all.at[n], sems.at[n, 1]),
        )

    shared = (
        pltpu.make_async_copy(proj_any, proj_ref, sems.at[steps, 0]),
        pltpu.make_async_copy(mats_any, mats_ref, sems.at[steps, 1]),
    )

    @pl.when(step == 0)
    def _():
        for copy in (shared[0], *loads(0), shared[1]):
            copy.start()
        for n in range(1, steps):
            for copy in loads(n):
                copy.start()
        for copy in shared:
            copy.wait()

    for n in range(steps):

        @pl.when(step == n)
        def _():
            for copy in loads(n):
                copy.wait()

    src_ref = src_all.at[step]
    tiles = width // TILE
    levels = mats_ref.shape[0]
    ang = ang_all[step].astype(F32)
    cos, sin = cos_sin(ang[:levels])
    proj = proj_ref[...]
    x = [dot(proj, src_ref[:, i * TILE : (i + 1) * TILE]).astype(BF) for i in range(tiles)]
    to = lax.broadcasted_iota(jnp.int32, (TILE, TILE), 1)
    frm = lax.broadcasted_iota(jnp.int32, (TILE, TILE), 0)
    for level in range(levels):
        span = 1 << level
        if span == 128:
            xp = [jnp.concatenate([v[:, 128:], v[:, :128]], axis=1) for v in x]
        else:
            perm = jnp.where(frm == (to ^ span), 1.0, 0.0).astype(BF)
            every = dot(jnp.concatenate(x, axis=0), perm).astype(BF)
            xp = [every[i * R : (i + 1) * R] for i in range(tiles)]
        mat = jnp.concatenate([mats_ref[level, 0], mats_ref[level, 1]], axis=1)
        c, s = row(cos, level), row(sin, level)
        x = [
            mix(mat, x[i], xp[i], c[:, i * TILE : (i + 1) * TILE], s[:, i * TILE : (i + 1) * TILE])
            for i in range(tiles)
        ]
    a = jnp.concatenate([ang[levels : levels + 6], jnp.zeros((2, ang.shape[1]), F32)], axis=0)
    for i in range(tiles):
        lo, mid, hi = i * TILE, i * TILE + 128, (i + 1) * TILE
        out_ref[i, :R] = x[i][:, :128]
        out_ref[i, R : 2 * R] = x[i][:, 128:]
        out_ref[i, 2 * R :] = jnp.concatenate([a[:, lo:mid], a[:, mid:hi]], axis=0).astype(BF)


def local_levels(steps, parts, start, before, source_field, angles, project_mats, local_mats):
    q, columns = source_field.shape
    width = columns // parts
    tiles = width // TILE
    args = [source_field, angles, project_mats, local_mats]
    if before is not None:
        args.append(before)
    return pl.pallas_call(
        functools.partial(local_kernel, start),
        grid=(steps,),
        in_specs=[pl.BlockSpec(memory_space=pltpu.HBM)] * len(args),
        out_specs=pl.BlockSpec((tiles, ROWS, 128), lambda i: (start + i, 0, 0)),
        out_shape=jax.ShapeDtypeStruct((BLOCKS, ROWS, 128), BF),
        scratch_shapes=[
            pltpu.VMEM((steps, q, width), BF),
            pltpu.VMEM((steps, angles.shape[0], width), BF),
            pltpu.VMEM(project_mats.shape, BF),
            pltpu.VMEM(local_mats.shape, BF),
            pltpu.SemaphoreType.DMA((steps + 1, 2)),
        ],
        input_output_aliases={4: 0} if before is not None else {},
        compiler_params=PARAMS,
    )(*args)


def phases_kernel(ang_ref, cos_ref, sin_ref):
    cos_ref[...], sin_ref[...] = cos_sin(ang_ref[...].astype(F32))


def phases(moved):
    out = jax.ShapeDtypeStruct((BLOCKS, 16, 128), F32)
    spec = pl.BlockSpec((BLOCKS, 16, 128), lambda i: (0, 0, 0))
    return pl.pallas_call(
        phases_kernel,
        grid=(1,),
        in_specs=[pl.BlockSpec((BLOCKS, 16, 128), lambda i: (0, 2 * R // 16, 0))],
        out_specs=[spec, spec],
        out_shape=[out, out],
        compiler_params=SMALL,
    )(moved)


def chip_kernel(data_ref, cos_ref, sin_ref, *refs):
    keep_ref, send_ref = refs[-2:]
    low = place()[2] == 0
    x, cs, last = {}, {}, {}
    for slot in SLOTS:
        block = block_of(slot)
        x[slot] = jnp.concatenate([data_ref[block, :R], data_ref[block, R : 2 * R]], axis=1)
        c, s = cos_ref[block], sin_ref[block]
        cs[slot] = (jnp.concatenate([c[:8], c[8:]], axis=1), jnp.concatenate([s[:8], s[8:]], axis=1))
        a = data_ref[block, 2 * R :].astype(F32)
        last[slot] = (a[:8], a[8:])
    flips = ((2, 0, 0), (1, 0, 0), (0, 2, 0), (0, 1, 0), (0, 0, 1))
    for level, flip in enumerate(flips):
        x = {
            (j, t, i): mix(
                refs[level // 3 * PLANES + t][j, level % 3, i],
                x[j, t, i],
                x[j ^ flip[0], t ^ flip[1], i ^ flip[2]],
                row(cs[j, t, i][0], level),
                row(cs[j, t, i][1], level),
            )
            for j, t, i in SLOTS
        }
    for n, slot in enumerate(SLOTS):
        at = n * R
        lo, hi = x[slot][:, :128], x[slot][:, 128:]
        keep_ref[at : at + R] = jnp.where(low, lo, hi)
        send_ref[at : at + R] = jnp.where(low, hi, lo)
    for n in range(0, BLOCKS, 2):
        at = BLOCKS * R + n * 8
        (lo0, hi0), (lo1, hi1) = last[SLOTS[n]], last[SLOTS[n + 1]]
        lo, hi = jnp.concatenate([lo0, lo1], axis=0), jnp.concatenate([hi0, hi1], axis=0)
        keep_ref[at : at + 16] = jnp.where(low, lo, hi).astype(BF)
        send_ref[at : at + 16] = jnp.where(low, hi, lo).astype(BF)
    for n, (j, t, i) in enumerate(SLOTS):
        at = BLOCKS * (R + 8) + n * R
        keep_ref[at : at + R] = refs[PLANES + t][j, 2, i]
        send_ref[at : at + R] = refs[PLANES + t][j, 2, i]


def chip_levels(moved, cos, sin, early, late):
    out = jax.ShapeDtypeStruct((BLOCKS * (2 * R + 8), 128), BF)
    vmem = pl.BlockSpec(memory_space=pltpu.VMEM)
    return pl.pallas_call(
        chip_kernel,
        in_specs=[vmem] * 11,
        out_specs=[vmem, vmem],
        out_shape=[out, out],
        compiler_params=SMALL,
    )(moved, cos, sin, *early, *late)


def last_kernel(own_ref, oth_ref, eval_ref, out_ref):
    low = place()[2] == 0
    ev = eval_ref[...]
    for n in range(BLOCKS):
        if n % 2 == 0:
            a = BLOCKS * R + n * 8
            own_c, own_s = cos_sin(own_ref[a : a + 16].astype(F32))
            oth_c, oth_s = cos_sin(oth_ref[a : a + 16].astype(F32))
        at, r, m = n * R, 5 + 8 * (n % 2), BLOCKS * (R + 8) + n * R
        own, oth = own_ref[at : at + R], oth_ref[at : at + R]
        y_own = mix(own_ref[m : m + R], own, oth, row(own_c, r), row(own_s, r))
        y_oth = mix(oth_ref[m : m + R], oth, own, row(oth_c, r), row(oth_s, r))
        y = jnp.concatenate([jnp.where(low, y_own, y_oth), jnp.where(low, y_oth, y_own)], axis=1)
        column = pl.multiple_of(block_of(SLOTS[n]) * TILE, TILE)
        out_ref[:, pl.ds(column, TILE)] = lax.dot_general(
            ev, y, (((0,), (0,)), ((), ())), preferred_element_type=F32
        ).astype(BF)


def last_level(keep, received, evaluate_mats):
    vmem = pl.BlockSpec(memory_space=pltpu.VMEM)
    return pl.pallas_call(
        last_kernel,
        in_specs=[vmem] * 3,
        out_specs=vmem,
        out_shape=jax.ShapeDtypeStruct((evaluate_mats.shape[1], 64 * 128), BF),
        compiler_params=SMALL,
    )(keep, received, evaluate_mats)


def shards(source_field, project_mats, local_mats, cross_mats, angles, evaluate_mats):
    count = NX * NZ * NC

    def swap(values, distance):
        return lax.ppermute(values, "box", [(i, i ^ distance) for i in range(count)])

    def to_plane(values):
        pairs = [(i * PLANES + p, (i ^ (2 * p * NC)) * PLANES + p) for i in range(count) for p in range(PLANES)]
        return lax.ppermute(values, ("box", "src"), pairs)

    def along_src(values, t):
        return lax.ppermute(values, "src", [(p, p ^ t) for p in range(PLANES)])

    def after(value, *first):
        return lax.optimization_barrier((value, *first))[0]

    chips = [[xx * NZ * NC + zz * NC + c for xx in range(NX) for zz in range(NZ)] for c in range(NC)]

    own = jnp.concatenate([cross_mats[:, 0], cross_mats[:, 1]], axis=-1)
    far = to_plane(own)
    first = local_levels(1, 2, 0, None, source_field, angles, project_mats, local_mats)
    far = after(far, first)
    near = swap(far, NC)
    far_x = [far] + [swap(far, j * NZ * NC) for j in (1, 3, 2)]
    near, half = lax.optimization_barrier((near, first))
    near_x = [near] + [swap(near, j * NZ * NC) for j in (1, 3, 2)]
    sent = local_levels(1, 2, 1, half, source_field, angles, project_mats, local_mats)
    sent, *pairs = lax.optimization_barrier((sent, *far_x, *near_x))
    moved = lax.all_to_all(sent, "box", 0, 0, tiled=True, axis_index_groups=chips)
    early, late = (
        jnp.stack([jnp.stack([pairs[j][p : p + 3], pairs[4 + j][p : p + 3]], axis=1) for j in (0, 1, 3, 2)])
        for p in (0, 3)
    )
    early3, late1 = along_src(early, 3), along_src(late, 1)
    early1, late3 = along_src(early, 1), along_src(late, 3)
    early2, late2 = along_src(early3, 1), along_src(late1, 3)

    keep, send = chip_levels(moved, *phases(moved), (early, early1, early2, early3), (late, late1, late2, late3))
    received = swap(send, 1)
    return last_level(keep, received, evaluate_mats.T)


def solution(mesh):
    in_specs = (
        P("src", "box"),
        P("box", None),
        P(None, None, "box", None),
        P(None, None, "box", None),
        P(None, "box"),
        P("box", None),
    )
    out_specs = P("src", "box")
    return jax.shard_map(shards, mesh=mesh, in_specs=in_specs, out_specs=out_specs, check_vma=False)
```

```python
import functools

import jax
import jax.numpy as jnp
from jax import lax
from jax.experimental import pallas as pl
from jax.experimental.pallas import tpu as pltpu
from jax.sharding import PartitionSpec as P

R = 64
TILE = 256
BF = jnp.bfloat16
F32 = jnp.float32

NX, NZ, NC, PLANES = 4, 8, 2, 4
BLOCKS = NX * NZ
ROWS = 2 * R + 16
PARAMS = pltpu.CompilerParams(vmem_limit_bytes=60 * 2**20)
SMALL = pltpu.CompilerParams(vmem_limit_bytes=24 * 2**20)
SLOTS = [(j, t, i) for j in range(NX) for t in range(PLANES) for i in range(2)]


def place():
    box = lax.axis_index("box")
    return box // (NZ * NC), box // NC % NZ, box % NC, lax.axis_index("src")


def block_of(slot):
    x, z, _, plane = place()
    j, t, i = slot
    return (x ^ j) * NZ + (z ^ (((plane ^ t) << 1) | i))


def dot(a, b):
    return jnp.dot(a, b, preferred_element_type=F32)


def cos_sin(t):
    h = 0.5 * t
    q = h * h
    s = 1.0 + q * (
        -1.0 / 6 + q * (1.0 / 120 + q * (-1.0 / 5040 + q * (1.0 / 362880 + q * (-1.0 / 39916800 + q * (1.0 / 6227020800)))))
    )
    s = s * h
    c = 1.0 + q * (
        -0.5 + q * (1.0 / 24 + q * (-1.0 / 720 + q * (1.0 / 40320 + q * (-1.0 / 3628800 + q * (1.0 / 479001600)))))
    )
    return 1.0 - 2.0 * s * s, 2.0 * s * c


def mix(mat, own, partner, c, s):
    return dot(mat, jnp.concatenate([own * c, partner * s], axis=0)).astype(BF)


def row(values, i):
    return values[i : i + 1].astype(BF)


def local_kernel(start, src_any, ang_any, proj_any, mats_any, *refs):
    out_ref, src_ref, ang_ref, proj_ref, mats_ref, sems = refs[-6:]
    width = src_ref.shape[1]
    half = width // 2
    halves = [
        pltpu.make_async_copy(
            src_any.at[:, pl.ds(start * width + n * half, half)], src_ref.at[:, pl.ds(n * half, half)], sems.at[n]
        )
        for n in range(2)
    ]
    of_proj = pltpu.make_async_copy(proj_any, proj_ref, sems.at[2])
    of_ang = pltpu.make_async_copy(ang_any.at[:, pl.ds(start * width, width)], ang_ref, sems.at[3])
    of_mats = pltpu.make_async_copy(mats_any, mats_ref, sems.at[4])
    for copy in (of_ang, of_proj, *halves, of_mats):
        copy.start()
    tiles = width // TILE
    levels = mats_ref.shape[0]
    of_ang.wait()
    ang = ang_ref[...].astype(F32)
    cos, sin = cos_sin(ang[:levels])
    of_proj.wait()
    proj = proj_ref[...]
    x = []
    for copy in halves:
        copy.wait()
        for _ in range(tiles // 2):
            i = len(x)
            x.append(dot(proj, src_ref[:, i * TILE : (i + 1) * TILE]).astype(BF))
    of_mats.wait()
    to = lax.broadcasted_iota(jnp.int32, (TILE, TILE), 1)
    frm = lax.broadcasted_iota(jnp.int32, (TILE, TILE), 0)
    for level in range(levels):
        span = 1 << level
        if span == 128:
            xp = [jnp.concatenate([v[:, 128:], v[:, :128]], axis=1) for v in x]
        else:
            perm = jnp.where(frm == (to ^ span), 1.0, 0.0).astype(BF)
            every = dot(jnp.concatenate(x, axis=0), perm).astype(BF)
            xp = [every[i * R : (i + 1) * R] for i in range(tiles)]
        mat = jnp.concatenate([mats_ref[level, 0], mats_ref[level, 1]], axis=1)
        c, s = row(cos, level), row(sin, level)
        x = [
            mix(mat, x[i], xp[i], c[:, i * TILE : (i + 1) * TILE], s[:, i * TILE : (i + 1) * TILE])
            for i in range(tiles)
        ]
    a = jnp.concatenate([ang[levels : levels + 6], jnp.zeros((2, ang.shape[1]), F32)], axis=0)
    for i in range(tiles):
        lo, mid, hi = i * TILE, i * TILE + 128, (i + 1) * TILE
        out_ref[i, :R] = x[i][:, :128]
        out_ref[i, R : 2 * R] = x[i][:, 128:]
        out_ref[i, 2 * R :] = jnp.concatenate([a[:, lo:mid], a[:, mid:hi]], axis=0).astype(BF)


def local_levels(parts, start, before, source_field, angles, project_mats, local_mats):
    q, columns = source_field.shape
    width = columns // parts
    tiles = width // TILE
    args = [source_field, angles, project_mats, local_mats]
    if before is not None:
        args.append(before)
    return pl.pallas_call(
        functools.partial(local_kernel, start),
        grid=(1,),
        in_specs=[pl.BlockSpec(memory_space=pltpu.HBM)] * len(args),
        out_specs=pl.BlockSpec((tiles, ROWS, 128), lambda i: (start + i, 0, 0)),
        out_shape=jax.ShapeDtypeStruct((BLOCKS, ROWS, 128), BF),
        scratch_shapes=[
            pltpu.VMEM((q, width), BF),
            pltpu.VMEM((angles.shape[0], width), BF),
            pltpu.VMEM(project_mats.shape, BF),
            pltpu.VMEM(local_mats.shape, BF),
            pltpu.SemaphoreType.DMA((5,)),
        ],
        input_output_aliases={4: 0} if before is not None else {},
        compiler_params=PARAMS,
    )(*args)


def phases_kernel(ang_ref, cos_ref, sin_ref):
    cos_ref[...], sin_ref[...] = cos_sin(ang_ref[...].astype(F32))


def phases(moved):
    out = jax.ShapeDtypeStruct((BLOCKS, 16, 128), F32)
    spec = pl.BlockSpec((BLOCKS, 16, 128), lambda i: (0, 0, 0))
    return pl.pallas_call(
        phases_kernel,
        grid=(1,),
        in_specs=[pl.BlockSpec((BLOCKS, 16, 128), lambda i: (0, 2 * R // 16, 0))],
        out_specs=[spec, spec],
        out_shape=[out, out],
        compiler_params=SMALL,
    )(moved)


def chip_kernel(data_ref, cos_ref, sin_ref, *refs):
    keep_ref, send_ref = refs[-2:]
    low = place()[2] == 0
    x, cs, last = {}, {}, {}
    for slot in SLOTS:
        block = block_of(slot)
        x[slot] = jnp.concatenate([data_ref[block, :R], data_ref[block, R : 2 * R]], axis=1)
        c, s = cos_ref[block], sin_ref[block]
        cs[slot] = (jnp.concatenate([c[:8], c[8:]], axis=1), jnp.concatenate([s[:8], s[8:]], axis=1))
        a = data_ref[block, 2 * R :].astype(F32)
        last[slot] = (a[:8], a[8:])
    flips = ((2, 0, 0), (1, 0, 0), (0, 2, 0), (0, 1, 0), (0, 0, 1))
    for level, flip in enumerate(flips):
        x = {
            (j, t, i): mix(
                refs[level // 3 * PLANES + t][j, level % 3, i],
                x[j, t, i],
                x[j ^ flip[0], t ^ flip[1], i ^ flip[2]],
                row(cs[j, t, i][0], level),
                row(cs[j, t, i][1], level),
            )
            for j, t, i in SLOTS
        }
    for n, slot in enumerate(SLOTS):
        at = n * R
        lo, hi = x[slot][:, :128], x[slot][:, 128:]
        keep_ref[at : at + R] = jnp.where(low, lo, hi)
        send_ref[at : at + R] = jnp.where(low, hi, lo)
    for n in range(0, BLOCKS, 2):
        at = BLOCKS * R + n * 8
        (lo0, hi0), (lo1, hi1) = last[SLOTS[n]], last[SLOTS[n + 1]]
        lo, hi = jnp.concatenate([lo0, lo1], axis=0), jnp.concatenate([hi0, hi1], axis=0)
        keep_ref[at : at + 16] = jnp.where(low, lo, hi).astype(BF)
        send_ref[at : at + 16] = jnp.where(low, hi, lo).astype(BF)
    for n, (j, t, i) in enumerate(SLOTS):
        at = BLOCKS * (R + 8) + n * R
        keep_ref[at : at + R] = refs[PLANES + t][j, 2, i]
        send_ref[at : at + R] = refs[PLANES + t][j, 2, i]


def chip_levels(moved, cos, sin, early, late):
    out = jax.ShapeDtypeStruct((BLOCKS * (2 * R + 8), 128), BF)
    vmem = pl.BlockSpec(memory_space=pltpu.VMEM)
    return pl.pallas_call(
        chip_kernel,
        in_specs=[vmem] * 11,
        out_specs=[vmem, vmem],
        out_shape=[out, out],
        compiler_params=SMALL,
    )(moved, cos, sin, *early, *late)


def last_kernel(own_ref, oth_ref, eval_ref, out_any, out_ref, sems):
    low = place()[2] == 0
    ev = eval_ref[...]
    copies = []
    for n in range(BLOCKS):
        if n % 2 == 0:
            a = BLOCKS * R + n * 8
            own_c, own_s = cos_sin(own_ref[a : a + 16].astype(F32))
            oth_c, oth_s = cos_sin(oth_ref[a : a + 16].astype(F32))
        at, r, m = n * R, 5 + 8 * (n % 2), BLOCKS * (R + 8) + n * R
        own, oth = own_ref[at : at + R], oth_ref[at : at + R]
        y_own = mix(own_ref[m : m + R], own, oth, row(own_c, r), row(own_s, r))
        y_oth = mix(oth_ref[m : m + R], oth, own, row(oth_c, r), row(oth_s, r))
        y = jnp.concatenate([jnp.where(low, y_own, y_oth), jnp.where(low, y_oth, y_own)], axis=1)
        column = pl.multiple_of(block_of(SLOTS[n]) * TILE, TILE)
        out_ref[:, pl.ds(column, TILE)] = lax.dot_general(
            ev, y, (((0,), (0,)), ((), ())), preferred_element_type=F32
        ).astype(BF)
        if n % (BLOCKS // NX) == BLOCKS // NX - 1:
            done = n // (BLOCKS // NX)
            columns = pl.ds(pl.multiple_of((place()[0] ^ done) * (NZ * TILE), NZ * TILE), NZ * TILE)
            copies.append(pltpu.make_async_copy(out_ref.at[:, columns], out_any.at[:, columns], sems.at[done]))
            copies[-1].start()
    for copy in copies:
        copy.wait()


def last_level(keep, received, evaluate_mats):
    vmem = pl.BlockSpec(memory_space=pltpu.VMEM)
    return pl.pallas_call(
        last_kernel,
        in_specs=[vmem] * 3,
        out_specs=pl.BlockSpec(memory_space=pl.ANY),
        out_shape=jax.ShapeDtypeStruct((evaluate_mats.shape[1], 64 * 128), BF),
        scratch_shapes=[pltpu.VMEM((evaluate_mats.shape[1], 64 * 128), BF), pltpu.SemaphoreType.DMA((NX,))],
        compiler_params=SMALL,
    )(keep, received, evaluate_mats)


def shards(source_field, project_mats, local_mats, cross_mats, angles, evaluate_mats):
    count = NX * NZ * NC

    def swap(values, distance):
        return lax.ppermute(values, "box", [(i, i ^ distance) for i in range(count)])

    def to_plane(values):
        pairs = [(i * PLANES + p, (i ^ (2 * p * NC)) * PLANES + p) for i in range(count) for p in range(PLANES)]
        return lax.ppermute(values, ("box", "src"), pairs)

    def along_src(values, t):
        return lax.ppermute(values, "src", [(p, p ^ t) for p in range(PLANES)])

    def after(value, *first):
        return lax.optimization_barrier((value, *first))[0]

    chips = [[xx * NZ * NC + zz * NC + c for xx in range(NX) for zz in range(NZ)] for c in range(NC)]

    own = jnp.concatenate([cross_mats[:, 0], cross_mats[:, 1]], axis=-1)
    far = to_plane(own)
    first = local_levels(2, 0, None, source_field, angles, project_mats, local_mats)
    far = after(far, first)
    near = swap(far, NC)
    far_x = [far] + [swap(far, j * NZ * NC) for j in (1, 3, 2)]
    near, half = lax.optimization_barrier((near, first))
    near_x = [near] + [swap(near, j * NZ * NC) for j in (1, 3, 2)]
    sent = local_levels(2, 1, half, source_field, angles, project_mats, local_mats)
    sent, *pairs = lax.optimization_barrier((sent, *far_x, *near_x))
    moved = lax.all_to_all(sent, "box", 0, 0, tiled=True, axis_index_groups=chips)
    early, late = (
        jnp.stack([jnp.stack([pairs[j][p : p + 3], pairs[4 + j][p : p + 3]], axis=1) for j in (0, 1, 3, 2)])
        for p in (0, 3)
    )
    early3, late1 = along_src(early, 3), along_src(late, 1)
    early1, late3 = along_src(early, 1), along_src(late, 3)
    early2, late2 = along_src(early3, 1), along_src(late1, 3)

    keep, send = chip_levels(moved, *phases(moved), (early, early1, early2, early3), (late, late1, late2, late3))
    received = swap(send, 1)
    return last_level(keep, received, evaluate_mats.T)


def solution(mesh):
    in_specs = (
        P("src", "box"),
        P("box", None),
        P(None, None, "box", None),
        P(None, None, "box", None),
        P(None, "box"),
        P("box", None),
    )
    out_specs = P("src", "box")
    return jax.shard_map(shards, mesh=mesh, in_specs=in_specs, out_specs=out_specs, check_vma=False)
```

```python
import functools

import jax
import jax.numpy as jnp
from jax import lax
from jax.experimental import pallas as pl
from jax.experimental.pallas import tpu as pltpu
from jax.sharding import PartitionSpec as P

R = 64
TILE = 256
BF = jnp.bfloat16
F32 = jnp.float32

NX, NZ, NC, PLANES = 4, 8, 2, 4
BLOCKS = NX * NZ
ROWS = 2 * R + 16
PARAMS = pltpu.CompilerParams(vmem_limit_bytes=60 * 2**20)
SMALL = pltpu.CompilerParams(vmem_limit_bytes=24 * 2**20)
SLOTS = [(j, t, i) for j in range(NX) for t in range(PLANES) for i in range(2)]


def place():
    box = lax.axis_index("box")
    return box // (NZ * NC), box // NC % NZ, box % NC, lax.axis_index("src")


def block_of(slot):
    x, z, _, plane = place()
    j, t, i = slot
    return (x ^ j) * NZ + (z ^ (((plane ^ t) << 1) | i))


def dot(a, b):
    return jnp.dot(a, b, preferred_element_type=F32)


def cos_sin(t):
    h = 0.5 * t
    q = h * h
    s = 1.0 + q * (
        -1.0 / 6 + q * (1.0 / 120 + q * (-1.0 / 5040 + q * (1.0 / 362880 + q * (-1.0 / 39916800 + q * (1.0 / 6227020800)))))
    )
    s = s * h
    c = 1.0 + q * (
        -0.5 + q * (1.0 / 24 + q * (-1.0 / 720 + q * (1.0 / 40320 + q * (-1.0 / 3628800 + q * (1.0 / 479001600)))))
    )
    return 1.0 - 2.0 * s * s, 2.0 * s * c


def mix(mat, own, partner, c, s):
    return dot(mat, jnp.concatenate([own * c, partner * s], axis=0)).astype(BF)


def row(values, i):
    return values[i : i + 1].astype(BF)


def swapped(values, span):
    if span == 64:
        return pltpu.roll(values, 64, 1)
    upper = (lax.broadcasted_iota(jnp.int32, values.shape, 1) & span) != 0
    return jnp.where(upper, pltpu.roll(values, span, 1), pltpu.roll(values, 128 - span, 1))


def local_kernel(start, src_any, ang_any, proj_any, mats_any, *refs):
    out_ref, src_ref, ang_ref, proj_ref, mats_ref, sems = refs[-6:]
    width = src_ref.shape[1]
    half = width // 2
    halves = [
        pltpu.make_async_copy(
            src_any.at[:, pl.ds(start * width + n * half, half)], src_ref.at[:, pl.ds(n * half, half)], sems.at[n]
        )
        for n in range(2)
    ]
    of_proj = pltpu.make_async_copy(proj_any, proj_ref, sems.at[2])
    of_ang = pltpu.make_async_copy(ang_any.at[:, pl.ds(start * width, width)], ang_ref, sems.at[3])
    of_mats = pltpu.make_async_copy(mats_any, mats_ref, sems.at[4])
    for copy in (of_ang, of_proj, *halves, of_mats):
        copy.start()
    tiles = width // TILE
    levels = mats_ref.shape[0]
    of_ang.wait()
    ang = ang_ref[...].astype(F32)
    cos, sin = cos_sin(ang[:levels])
    of_proj.wait()
    proj = proj_ref[...]
    x = []
    for copy in halves:
        copy.wait()
        for _ in range(tiles // 2):
            i = len(x)
            x.append(dot(proj, src_ref[:, i * TILE : (i + 1) * TILE]).astype(BF))
    of_mats.wait()
    to = lax.broadcasted_iota(jnp.int32, (TILE, TILE), 1)
    frm = lax.broadcasted_iota(jnp.int32, (TILE, TILE), 0)
    for level in range(levels):
        span = 1 << level
        if span == 128:
            xp = [jnp.concatenate([v[:, 128:], v[:, :128]], axis=1) for v in x]
        else:
            perm = jnp.where(frm == (to ^ span), 1.0, 0.0).astype(BF)
            product = tiles - tiles // 3
            every = dot(jnp.concatenate(x[:product], axis=0), perm).astype(BF)
            xp = [every[i * R : (i + 1) * R] for i in range(product)]
            xp += [jnp.concatenate([swapped(v[:, :128], span), swapped(v[:, 128:], span)], axis=1) for v in x[product:]]
        mat = jnp.concatenate([mats_ref[level, 0], mats_ref[level, 1]], axis=1)
        c, s = row(cos, level), row(sin, level)
        x = [
            mix(mat, x[i], xp[i], c[:, i * TILE : (i + 1) * TILE], s[:, i * TILE : (i + 1) * TILE])
            for i in range(tiles)
        ]
    a = jnp.concatenate([ang[levels : levels + 6], jnp.zeros((2, ang.shape[1]), F32)], axis=0)
    for i in range(tiles):
        lo, mid, hi = i * TILE, i * TILE + 128, (i + 1) * TILE
        out_ref[i, :R] = x[i][:, :128]
        out_ref[i, R : 2 * R] = x[i][:, 128:]
        out_ref[i, 2 * R :] = jnp.concatenate([a[:, lo:mid], a[:, mid:hi]], axis=0).astype(BF)


def local_levels(parts, start, before, source_field, angles, project_mats, local_mats):
    q, columns = source_field.shape
    width = columns // parts
    tiles = width // TILE
    args = [source_field, angles, project_mats, local_mats]
    if before is not None:
        args.append(before)
    return pl.pallas_call(
        functools.partial(local_kernel, start),
        grid=(1,),
        in_specs=[pl.BlockSpec(memory_space=pltpu.HBM)] * len(args),
        out_specs=pl.BlockSpec((tiles, ROWS, 128), lambda i: (start + i, 0, 0)),
        out_shape=jax.ShapeDtypeStruct((BLOCKS, ROWS, 128), BF),
        scratch_shapes=[
            pltpu.VMEM((q, width), BF),
            pltpu.VMEM((angles.shape[0], width), BF),
            pltpu.VMEM(project_mats.shape, BF),
            pltpu.VMEM(local_mats.shape, BF),
            pltpu.SemaphoreType.DMA((5,)),
        ],
        input_output_aliases={4: 0} if before is not None else {},
        compiler_params=PARAMS,
    )(*args)


def phases_kernel(ang_ref, cos_ref, sin_ref):
    cos_ref[...], sin_ref[...] = cos_sin(ang_ref[...].astype(F32))


def phases(moved):
    out = jax.ShapeDtypeStruct((BLOCKS, 16, 128), F32)
    spec = pl.BlockSpec((BLOCKS, 16, 128), lambda i: (0, 0, 0))
    return pl.pallas_call(
        phases_kernel,
        grid=(1,),
        in_specs=[pl.BlockSpec((BLOCKS, 16, 128), lambda i: (0, 2 * R // 16, 0))],
        out_specs=[spec, spec],
        out_shape=[out, out],
        compiler_params=SMALL,
    )(moved)


def chip_kernel(data_ref, cos_ref, sin_ref, *refs):
    keep_ref, send_ref = refs[-2:]
    low = place()[2] == 0
    x, cs, last = {}, {}, {}
    for slot in SLOTS:
        block = block_of(slot)
        x[slot] = jnp.concatenate([data_ref[block, :R], data_ref[block, R : 2 * R]], axis=1)
        c, s = cos_ref[block], sin_ref[block]
        cs[slot] = (jnp.concatenate([c[:8], c[8:]], axis=1), jnp.concatenate([s[:8], s[8:]], axis=1))
        a = data_ref[block, 2 * R :].astype(F32)
        last[slot] = (a[:8], a[8:])
    flips = ((2, 0, 0), (1, 0, 0), (0, 2, 0), (0, 1, 0), (0, 0, 1))
    for level, flip in enumerate(flips):
        x = {
            (j, t, i): mix(
                refs[level // 3 * PLANES + t][j, level % 3, i],
                x[j, t, i],
                x[j ^ flip[0], t ^ flip[1], i ^ flip[2]],
                row(cs[j, t, i][0], level),
                row(cs[j, t, i][1], level),
            )
            for j, t, i in SLOTS
        }
    for n, slot in enumerate(SLOTS):
        at = n * R
        lo, hi = x[slot][:, :128], x[slot][:, 128:]
        keep_ref[at : at + R] = jnp.where(low, lo, hi)
        send_ref[at : at + R] = jnp.where(low, hi, lo)
    for n in range(0, BLOCKS, 2):
        at = BLOCKS * R + n * 8
        (lo0, hi0), (lo1, hi1) = last[SLOTS[n]], last[SLOTS[n + 1]]
        lo, hi = jnp.concatenate([lo0, lo1], axis=0), jnp.concatenate([hi0, hi1], axis=0)
        keep_ref[at : at + 16] = jnp.where(low, lo, hi).astype(BF)
        send_ref[at : at + 16] = jnp.where(low, hi, lo).astype(BF)
    for n, (j, t, i) in enumerate(SLOTS):
        at = BLOCKS * (R + 8) + n * R
        keep_ref[at : at + R] = refs[PLANES + t][j, 2, i]
        send_ref[at : at + R] = refs[PLANES + t][j, 2, i]


def chip_levels(moved, cos, sin, early, late):
    out = jax.ShapeDtypeStruct((BLOCKS * (2 * R + 8), 128), BF)
    vmem = pl.BlockSpec(memory_space=pltpu.VMEM)
    return pl.pallas_call(
        chip_kernel,
        in_specs=[vmem] * 11,
        out_specs=[vmem, vmem],
        out_shape=[out, out],
        compiler_params=SMALL,
    )(moved, cos, sin, *early, *late)


def last_kernel(own_ref, oth_ref, eval_ref, out_any, out_ref, sems):
    low = place()[2] == 0
    ev = eval_ref[...]
    copies = []
    for n in range(BLOCKS):
        if n % 2 == 0:
            a = BLOCKS * R + n * 8
            own_c, own_s = cos_sin(own_ref[a : a + 16].astype(F32))
            oth_c, oth_s = cos_sin(oth_ref[a : a + 16].astype(F32))
        at, r, m = n * R, 5 + 8 * (n % 2), BLOCKS * (R + 8) + n * R
        own, oth = own_ref[at : at + R], oth_ref[at : at + R]
        y_own = mix(own_ref[m : m + R], own, oth, row(own_c, r), row(own_s, r))
        y_oth = mix(oth_ref[m : m + R], oth, own, row(oth_c, r), row(oth_s, r))
        y = jnp.concatenate([jnp.where(low, y_own, y_oth), jnp.where(low, y_oth, y_own)], axis=1)
        column = pl.multiple_of(block_of(SLOTS[n]) * TILE, TILE)
        out_ref[:, pl.ds(column, TILE)] = lax.dot_general(
            ev, y, (((0,), (0,)), ((), ())), preferred_element_type=F32
        ).astype(BF)
        if n % (BLOCKS // NX) == BLOCKS // NX - 1:
            done = n // (BLOCKS // NX)
            columns = pl.ds(pl.multiple_of((place()[0] ^ done) * (NZ * TILE), NZ * TILE), NZ * TILE)
            copies.append(pltpu.make_async_copy(out_ref.at[:, columns], out_any.at[:, columns], sems.at[done]))
            copies[-1].start()
    for copy in copies:
        copy.wait()


def last_level(keep, received, evaluate_mats):
    vmem = pl.BlockSpec(memory_space=pltpu.VMEM)
    return pl.pallas_call(
        last_kernel,
        in_specs=[vmem] * 3,
        out_specs=pl.BlockSpec(memory_space=pl.ANY),
        out_shape=jax.ShapeDtypeStruct((evaluate_mats.shape[1], 64 * 128), BF),
        scratch_shapes=[pltpu.VMEM((evaluate_mats.shape[1], 64 * 128), BF), pltpu.SemaphoreType.DMA((NX,))],
        compiler_params=SMALL,
    )(keep, received, evaluate_mats)


def shards(source_field, project_mats, local_mats, cross_mats, angles, evaluate_mats):
    count = NX * NZ * NC

    def swap(values, distance):
        return lax.ppermute(values, "box", [(i, i ^ distance) for i in range(count)])

    def to_plane(values):
        pairs = [(i * PLANES + p, (i ^ (2 * p * NC)) * PLANES + p) for i in range(count) for p in range(PLANES)]
        return lax.ppermute(values, ("box", "src"), pairs)

    def along_src(values, t):
        return lax.ppermute(values, "src", [(p, p ^ t) for p in range(PLANES)])

    def after(value, *first):
        return lax.optimization_barrier((value, *first))[0]

    chips = [[xx * NZ * NC + zz * NC + c for xx in range(NX) for zz in range(NZ)] for c in range(NC)]

    own = jnp.concatenate([cross_mats[:, 0], cross_mats[:, 1]], axis=-1)
    far = to_plane(own)
    first = local_levels(2, 0, None, source_field, angles, project_mats, local_mats)
    far = after(far, first)
    near = swap(far, NC)
    far_x = [far] + [swap(far, j * NZ * NC) for j in (1, 3, 2)]
    near, half = lax.optimization_barrier((near, first))
    near_x = [near] + [swap(near, j * NZ * NC) for j in (1, 3, 2)]
    sent = local_levels(2, 1, half, source_field, angles, project_mats, local_mats)
    sent, *pairs = lax.optimization_barrier((sent, *far_x, *near_x))
    moved = lax.all_to_all(sent, "box", 0, 0, tiled=True, axis_index_groups=chips)
    early, late = (
        jnp.stack([jnp.stack([pairs[j][p : p + 3], pairs[4 + j][p : p + 3]], axis=1) for j in (0, 1, 3, 2)])
        for p in (0, 3)
    )
    early3, late1 = along_src(early, 3), along_src(late, 1)
    early1, late3 = along_src(early, 1), along_src(late, 3)
    early2, late2 = along_src(early3, 1), along_src(late1, 3)

    keep, send = chip_levels(moved, *phases(moved), (early, early1, early2, early3), (late, late1, late2, late3))
    received = swap(send, 1)
    return last_level(keep, received, evaluate_mats.T)


def solution(mesh):
    in_specs = (
        P("src", "box"),
        P("box", None),
        P(None, None, "box", None),
        P(None, None, "box", None),
        P(None, "box"),
        P("box", None),
    )
    out_specs = P("src", "box")
    return jax.shard_map(shards, mesh=mesh, in_specs=in_specs, out_specs=out_specs, check_vma=False)
```
